128 devices in a mesh: row: 16 (over z, x_hi, core), col: 8 (over y, x_lo).
Axes of the slice: x: 4 (x_hi: 2, x_lo: 2; x = x_hi * 2 + x_lo), y: 4, z: 4, core: 2. Of those that a mesh axis runs over, the one named last changes fastest.
Arguments:
- tensor: float32 [1024, 8, 24576], P('row', 'col'), may hold values from -6 to 6
- occupancy: int32 [16, 8, 384], P('row', 'col'), may hold values 0 or 1
- coefficients: float32 [24576, 3072], P('row', 'col'), may hold values from -0.0390625 to 0.0390625
- coeff_occupancy: int32 [384, 48], P('row', 'col'), may hold values 0 or 1
Outputs:
- transformed: float32 [1024, 8, 3072], P('row', 'col')
The draws below stay inside these ranges and needn't reach their ends.
All inputs are finite; a program needn't handle non-finite values. No bound on the sum of `occupancy` or of `coeff_occupancy` on one device may be relied on, other than what follows from the above.
Results may differ from the reference program's by a relative error of at most 0.00015.
Values sent between devices are 32-bit elements; how exact they have to be, the bound alone decides.
A program may use at most 128 MiB of HBM per device.

```python
import jax
import jax.numpy as jnp
from jax import lax

BLOCK = 64
NU = 24576
OCC = 3072
MU = 1024
P_SIZE = 8


def set_ends(values, key, least, largest):
    longest = values.shape.index(max(values.shape))
    spots = []
    for shift in (0, 1):
        where = [jax.random.randint(jax.random.fold_in(key, axis), (), 0, length) for axis, length in enumerate(values.shape)]
        where[longest] = (where[longest] + shift) % values.shape[longest]
        spots.append(tuple(where))
    return values.at[spots[0]].set(least).at[spots[1]].set(largest)


def raised(entries, own_key, source, target, parts, factor):
    owner, partner = [(jnp.arange(entries.shape[dim]) // (entries.shape[dim] // parts)).reshape([-1 if axis == dim else 1 for axis in range(entries.ndim)]) for dim in (source, target)]
    chosen = jax.random.permutation(own_key, parts)[partner]
    strong = (owner == chosen) | (owner == (partner + parts // 2) % parts)
    return jnp.where(strong, factor * entries, entries)


def shard_levels(rng, shape, shards, smallest, top_value):
    def one(position, parts):
        steps = jax.random.uniform(jax.random.fold_in(jax.random.fold_in(rng, 6), position), (parts,), jnp.float32, smallest / len(shards), top_value / len(shards))
        return jnp.repeat(jnp.exp(steps), shape[position] // parts).reshape((-1,) + (1,) * (len(shape) - position - 1))

    level = one(*shards[0])
    for cut in shards[1:]:
        level = level * one(*cut)
    return level


def bell_draw(key, dims, width, limit, split=(), kind=jnp.bfloat16):
    loudness = shard_levels(key, dims, split, -0.22, 0.18) if split else 1.0
    drawn = jax.random.normal(key, dims, jnp.float32) * width * loudness
    return jnp.minimum(jnp.maximum(drawn, -limit), limit).astype(kind)


def heavy_noise(own_key, shape, spread, most, split, heavy, held_as=jnp.bfloat16):
    entries = spread * jax.random.normal(own_key, shape, jnp.float32)
    if split:
        entries = entries * shard_levels(own_key, shape, split, -0.22, 0.18)
    return jnp.clip(raised(entries, jax.random.fold_in(own_key, 3), *heavy), -most, most).astype(held_as)


def setup_inputs(seed: int = 0) -> dict:
    arg_keys = jax.random.split(jax.random.key(seed), 5)
    tensor = heavy_noise(arg_keys[0], (MU, P_SIZE, NU), 1.0, 6.0, ((0, 16), (1, 8)), (2, 0, 16, 2.0), jnp.float32)
    occupancy = set_ends((jax.random.randint(arg_keys[1], (MU // BLOCK, P_SIZE, NU // BLOCK), 0, 2) < 1).astype(jnp.int32), jax.random.fold_in(arg_keys[1], 1), 0, 1)
    coefficients = bell_draw(arg_keys[2], (NU, OCC), NU ** -0.5, 0.0390625, ((0, 16), (1, 8)), jnp.float32)
    coeff_occupancy = set_ends((jax.random.randint(arg_keys[3], (NU // BLOCK, OCC // BLOCK), 0, 3) < 2).astype(jnp.int32), jax.random.fold_in(arg_keys[3], 1), 0, 1)
    return {"tensor": tensor, "occupancy": occupancy, "coefficients": coefficients, "coeff_occupancy": coeff_occupancy}


def reference(tensor, occupancy, coefficients, coeff_occupancy):
    coeff_mask = jnp.repeat(jnp.repeat(coeff_occupancy.astype(jnp.float32), BLOCK, axis=0), BLOCK, axis=1)
    masked_coeff = coefficients * coeff_mask

    def one_function(index):
        slab = lax.dynamic_index_in_dim(tensor, index, 1, keepdims=False)
        blocks = lax.dynamic_index_in_dim(occupancy, index, 1, keepdims=False).astype(jnp.float32)
        expanded = jnp.repeat(jnp.repeat(blocks, BLOCK, axis=0), BLOCK, axis=1)
        return jnp.dot(slab * expanded, masked_coeff, preferred_element_type=jnp.float32, precision=lax.Precision.HIGHEST)

    stacked = lax.map(one_function, jnp.arange(P_SIZE, dtype=jnp.int32))
    return jnp.transpose(stacked, (1, 0, 2))
```

```python
import functools

import jax
import jax.numpy as jnp
from jax import lax
from jax.experimental import pallas as pl
from jax.experimental.pallas import tpu as pltpu
from jax.sharding import PartitionSpec as P

BLOCK = 64
MESH = pl.DeviceIdType.MESH
PIECES = 4
OFFSETS = [(ez, eh, ec) for eh in range(2) for ec in range(2) for ez in range(4)]
PANELS = [(0, 0), (0, 1), (3, 0), (1, 0), (3, 1), (1, 1), (2, 0), (2, 1)]
TASKS = [(0, 0), (1, 0), (2, 0), (3, 0), (0, 1), (1, 1), (2, 1), (3, 1),
         (4, 0), (4, 1), (5, 0), (5, 1), (6, 0), (6, 1), (7, 0), (7, 1)]


def place(offset):
    ez, eh, ec = offset
    return eh * 8 + ec * 4 + ez


def opposite(offset):
    ez, eh, ec = offset
    return ((4 - ez) % 4, eh, ec)


def kernel(a_hbm, amask, b_hbm, bmask, out_ref, astage, arecv, ahi, alo, bbuf, bhi, blo, cpart, crecv, zrecv, keep, xrecv,
           al_sem, as_sem, ar_sem, bl_sem, bs_sem, br_sem, cs_sem, cr_sem, zs_sem, zr_sem, xs_sem, xr_sem):
    depth, width = bbuf.shape[1:]
    chunk = depth // PIECES
    r, c = lax.axis_index("row"), lax.axis_index("col")
    z, xh, core = r // 4, (r // 2) % 2, r % 2
    y, xl = c // 2, c % 2

    def row_of(offset):
        ez, eh, ec = offset
        return ((z + ez) % 4) * 4 + ((xh + eh) % 2) * 2 + (core + ec) % 2

    def col_of(ey, el):
        return ((y + ey) % 4) * 2 + (xl + el) % 2

    def remote(src, dst, send, recv, device):
        return pltpu.make_async_remote_copy(src_ref=src, dst_ref=dst, send_sem=send, recv_sem=recv,
                                            device_id=device, device_id_type=MESH)

    up, down, pair = (r, col_of(1, 0)), (r, col_of(3, 0)), (r, col_of(0, 1))

    def b_load(k):
        rows = pl.ds(k * chunk, chunk)
        return pltpu.make_async_copy(b_hbm.at[rows], bbuf.at[0, rows], bl_sem.at[k])

    def a_load(offset):
        i = place(offset)
        cols = pl.ds(pl.multiple_of(row_of(offset) * depth, 128), depth)
        return pltpu.make_async_copy(a_hbm.at[:, cols], astage.at[i], al_sem.at[i])

    order = (0, 2, 1, 3)
    for k in order:
        b_load(k).start()
    send_order = sorted(OFFSETS, key=lambda o: (o[1] == 0, o[0] == 0, o[2]))
    for offset in send_order:
        a_load(offset).start()

    barrier = pltpu.get_barrier_semaphore()
    partners = [(row_of(o), c) for o in OFFSETS[1:]] + [up, down, pair]
    for device in partners:
        pl.semaphore_signal(barrier, inc=1, device_id=device, device_id_type=MESH)
    pl.semaphore_wait(barrier, len(partners))

    def b_copy(src, dst, k, device, sends):
        rows = pl.ds(k * chunk, chunk)
        return remote(bbuf.at[src, rows], bbuf.at[dst, rows], bs_sem.at[sends, k], br_sem.at[dst, k], device)

    own_up = [b_copy(0, 2, k, up, 0) for k in range(PIECES)]
    own_down = [b_copy(0, 3, k, down, 1) for k in range(PIECES)]
    own_pair = [b_copy(0, 1, k, pair, 2) for k in range(PIECES)]
    pair_up = [b_copy(1, 4, k, up, 3) for k in range(PIECES)]
    pair_down = [b_copy(1, 5, k, down, 4) for k in range(PIECES)]
    half = PIECES // 2
    on_own = [b_copy(2, 6, k, up, 5) if k < half else b_copy(3, 6, k, down, 5) for k in range(PIECES)]
    on_pair = [b_copy(4, 7, k, up, 6) if k < half else b_copy(5, 7, k, down, 6) for k in range(PIECES)]

    per = chunk // BLOCK
    for k in order:
        b_load(k).wait()
        for j in range(per):
            rows = pl.ds(k * chunk + j * BLOCK, BLOCK)
            bbuf[0, rows, :] = bbuf[0, rows, :] * bmask[k * per + j:k * per + j + 1, :]
        own_pair[k].start()
        own_up[k].start()
        own_down[k].start()

    def a_copy(offset):
        i, j = place(offset), place(opposite(offset))
        return remote(astage.at[i], arecv.at[j], as_sem.at[i], ar_sem.at[j], (row_of(offset), c))

    def split(values, i):
        high = values.astype(jnp.bfloat16)
        rows = pl.ds(i * BLOCK, BLOCK)
        ahi[rows, :] = high
        alo[rows, :] = (values - high.astype(jnp.float32)).astype(jnp.bfloat16)

    for offset in send_order:
        i = place(offset)
        a_load(offset).wait()
        masked = astage[i] * amask[pl.ds(row_of(offset), 1), :]
        if i == 0:
            split(masked, 0)
        else:
            astage[i] = masked
            a_copy(offset).start()

    def take(h):
        for offset in OFFSETS:
            i = place(offset)
            if i > 0 and offset[1] == h:
                a_copy(opposite(offset)).wait_recv()
                split(arecv[i], i)

    def multiply(t):
        n, h = TASKS[t]
        slot = t % 2
        if t >= 2:
            c_copy(t - 2).wait_send()

        def convert(j, _):
            rows = pl.ds(pl.multiple_of(j * BLOCK, BLOCK), BLOCK)
            values = bbuf[n, rows, :]
            high = values.astype(jnp.bfloat16)
            bhi[rows, :] = high
            blo[rows, :] = (values - high.astype(jnp.float32)).astype(jnp.bfloat16)
            return _

        lax.fori_loop(0, depth // BLOCK, convert, 0)

        def tile(m, _):
            rows = pl.ds(pl.multiple_of(h * 512 + m * 256, 256), 256)
            high, low = ahi[rows, :], alo[rows, :]
            total = jnp.dot(low, bhi[...], preferred_element_type=jnp.float32)
            total += jnp.dot(high, blo[...], preferred_element_type=jnp.float32)
            total += jnp.dot(high, bhi[...], preferred_element_type=jnp.float32)
            cpart[slot, pl.ds(m * 4, 4)] = total.reshape(4, BLOCK, width)
            return _

        lax.fori_loop(0, 2, tile, 0)
        c_copy(t).start()

    other = (row_of((0, 0, 1)), c)

    def c_copy(t):
        return remote(cpart.at[t % 2, pl.ds(4, 4)], crecv.at[t], cs_sem.at[t], cr_sem.at[t], other)

    def z_copy(t, ez):
        return remote(crecv.at[t, ez], zrecv.at[t, ez - 1], zs_sem.at[t, ez - 1], zr_sem.at[t, ez - 1],
                      (row_of((ez, 0, 0)), c))

    def x_copy(t):
        n = TASKS[t][0]
        return remote(keep.at[1, n], xrecv.at[n], xs_sem.at[n], xr_sem.at[n], (row_of((0, 1, 0)), c))

    def over_cores(t):
        c_copy(t).wait_recv()
        crecv[t] = crecv[t] + cpart[t % 2, pl.ds(0, 4)]
        for ez in (2, 1, 3):
            z_copy(t, ez).start()

    def over_z(t):
        n, h = TASKS[t]
        for ez in (1, 2, 3):
            z_copy(t, ez).wait_recv()
        keep[h, n] = (crecv[t, 0] + zrecv[t, 0]) + (zrecv[t, 1] + zrecv[t, 2])
        if h == 1:
            x_copy(t).start()

    def finish(t):
        n, h = TASKS[t]
        if h == 0:
            return
        x_copy(t).wait_recv()
        cols = pl.ds(pl.multiple_of(col_of(*PANELS[n]) * width, 128), width)
        out_ref[:, cols] = keep[0, n] + xrecv[n]

    def forward_own():
        for k in (0, 2, 1, 3):
            (own_up if k < half else own_down)[k].wait_recv()
            on_own[k].start()

    def forward_pair():
        for k in order:
            own_pair[k].wait_recv()
            pair_up[k].start()
            pair_down[k].start()

    def pass_on_pair():
        for k in (0, 2, 1, 3):
            (pair_up if k < half else pair_down)[k].wait_recv()
            on_pair[k].start()

    def rest(copies, ks):
        for k in ks:
            copies[k].wait_recv()

    before = {
        0: lambda: (forward_own(), take(0)),
        1: forward_pair,
        2: lambda: rest(own_up, range(half, PIECES)),
        3: lambda: rest(own_down, range(half)),
        4: lambda: take(1),
        8: lambda: (pass_on_pair(), rest(pair_up, range(half, PIECES))),
        10: lambda: rest(pair_down, range(half)),
        12: lambda: rest(on_own, range(PIECES)),
        14: lambda: rest(on_pair, range(PIECES)),
    }
    count = len(TASKS)
    for t in range(count + 4):
        if t in before:
            before[t]()
        if t < count:
            multiply(t)
        if 0 <= t - 1 < count:
            over_cores(t - 1)
        if 0 <= t - 2 < count:
            over_z(t - 2)
        if 0 <= t - 4 < count:
            finish(t - 4)

    for copies in (own_up, own_down, own_pair, pair_up, pair_down, on_own, on_pair):
        for copy in copies:
            copy.wait_send()
    for offset in OFFSETS[1:]:
        a_copy(offset).wait_send()
    for t in (count - 2, count - 1):
        c_copy(t).wait_send()
    for t in range(count):
        for ez in (1, 2, 3):
            z_copy(t, ez).wait_send()
        if TASKS[t][1] == 1:
            x_copy(t).wait_send()


def on_device(tensor, occupancy, coefficients, coeff_occupancy):
    mu_dev, p_dev, nu_all = tensor.shape
    depth, width = coefficients.shape
    count = nu_all // depth
    amask = jnp.repeat(occupancy.astype(jnp.float32).reshape(count, depth // BLOCK), BLOCK, axis=1)
    bmask = jnp.repeat(coeff_occupancy.astype(jnp.float32), BLOCK, axis=1)
    panels, tasks = len(PANELS), len(TASKS)
    f32, bf16, dma = jnp.float32, jnp.bfloat16, pltpu.SemaphoreType.DMA
    vmem, hbm = pl.BlockSpec(memory_space=pltpu.VMEM), pl.BlockSpec(memory_space=pl.ANY)
    result = pl.pallas_call(
        kernel,
        out_shape=jax.ShapeDtypeStruct((mu_dev, panels * width), f32),
        in_specs=[hbm, vmem, hbm, vmem],
        out_specs=vmem,
        scratch_shapes=[
            pltpu.VMEM((count, mu_dev, depth), f32),
            pltpu.VMEM((count, mu_dev, depth), f32),
            pltpu.VMEM((count * mu_dev, depth), bf16),
            pltpu.VMEM((count * mu_dev, depth), bf16),
            pltpu.VMEM((panels, depth, width), f32),
            pltpu.VMEM((depth, width), bf16),
            pltpu.VMEM((depth, width), bf16),
            pltpu.VMEM((2, 8, mu_dev, width), f32),
            pltpu.VMEM((tasks, 4, mu_dev, width), f32),
            pltpu.VMEM((tasks, 3, mu_dev, width), f32),
            pltpu.VMEM((2, panels, mu_dev, width), f32),
            pltpu.VMEM((panels, mu_dev, width), f32),
            dma((count,)), dma((count,)), dma((count,)),
            dma((PIECES,)), dma((7, PIECES)), dma((panels, PIECES)),
            dma((tasks,)), dma((tasks,)), dma((tasks, 3)), dma((tasks, 3)),
            dma((panels,)), dma((panels,)),
        ],
        compiler_params=pltpu.CompilerParams(
            collective_id=0, has_side_effects=True, vmem_limit_bytes=62 * 1024 * 1024),
        cost_estimate=pl.CostEstimate(
            flops=6 * count * mu_dev * depth * panels * width, bytes_accessed=16 * 1024 * 1024, transcendentals=0),
        name="transform",
    )(tensor.reshape(mu_dev * p_dev, nu_all), amask, coefficients, bmask)
    return result.reshape(mu_dev, p_dev, panels * width)


def solution(mesh):
    in_specs = (P("row", "col", None), P("row", "col", None), P("row", "col"), P("row", "col"))
    out_specs = P("row", "col", None)
    return jax.shard_map(
        on_device, mesh=mesh, in_specs=in_specs, out_specs=out_specs, check_vma=False
    )
```

```python
import functools

import jax
import jax.numpy as jnp
from jax import lax
from jax.experimental import pallas as pl
from jax.experimental.pallas import tpu as pltpu
from jax.sharding import PartitionSpec as P

BLOCK = 64
MESH = pl.DeviceIdType.MESH
PIECES = 4
SLOTS = 3
CORE_LAG = 1
PASS_LAG = 3
Z_LAG = 5
X_LAG = 7
OFFSETS = [(ez, eh, ec) for eh in range(2) for ec in range(2) for ez in range(4)]
PANELS = [(0, 0), (0, 1), (3, 0), (1, 0), (3, 1), (1, 1), (2, 0), (2, 1)]
TASKS = [(0, 0), (2, 0), (3, 0), (1, 0), (6, 0), (0, 1), (2, 1), (3, 1), (1, 1), (6, 1),
         (4, 0), (4, 1), (5, 0), (5, 1), (7, 1), (7, 0)]


def place(offset):
    ez, eh, ec = offset
    return eh * 8 + ec * 4 + ez


def opposite(offset):
    ez, eh, ec = offset
    return ((4 - ez) % 4, eh, ec)


def kernel(a_hbm, aocc, b_hbm, bocc, out_ref, araw, astage, arecv, ahi, alo, bbuf, bhi, blo, cpart, crecv, zrecv, keep, xrecv,
           al_sem, as_sem, ar_sem, bl_sem, bs_sem, br_sem, cs_sem, cr_sem, zs_sem, zr_sem, xs_sem, xr_sem):
    depth, width = bbuf.shape[1:]
    chunk = depth // PIECES
    r, c = lax.axis_index("row"), lax.axis_index("col")
    z, xh, core = r // 4, (r // 2) % 2, r % 2
    y, xl = c // 2, c % 2

    def row_of(offset):
        ez, eh, ec = offset
        return ((z + ez) % 4) * 4 + ((xh + eh) % 2) * 2 + (core + ec) % 2

    def col_of(ey, el):
        return ((y + ey) % 4) * 2 + (xl + el) % 2

    def remote(src, dst, send, recv, device):
        return pltpu.make_async_remote_copy(src_ref=src, dst_ref=dst, send_sem=send, recv_sem=recv,
                                            device_id=device, device_id_type=MESH)

    up, down, pair = (r, col_of(1, 0)), (r, col_of(3, 0)), (r, col_of(0, 1))

    def b_load(k):
        rows = pl.ds(k * chunk, chunk)
        return pltpu.make_async_copy(b_hbm.at[rows], bbuf.at[0, rows], bl_sem.at[k])

    strips = depth // 128
    chips = [(2, 0), (1, 0), (3, 0), (0, 0), (2, 1), (1, 1), (3, 1), (0, 1)]

    def a_load(j):
        ez, eh = chips[j]
        rows = pl.ds(pl.multiple_of(row_of((ez, eh, 0)) // 2 * 2 * strips, 8), 2 * strips)
        return pltpu.make_async_copy(a_hbm.at[:, rows], araw.at[j % SLOTS], al_sem.at[j])

    order = (0, 2, 1, 3)
    for k in order:
        b_load(k).start()
    for j in range(SLOTS):
        a_load(j).start()

    barrier = pltpu.get_barrier_semaphore()
    partners = [(row_of(o), c) for o in OFFSETS[1:]] + [up, down, pair]
    for device in partners:
        pl.semaphore_signal(barrier, inc=1, device_id=device, device_id_type=MESH)
    pl.semaphore_wait(barrier, len(partners))

    def b_copy(src, dst, k, device, sends):
        rows = pl.ds(k * chunk, chunk)
        return remote(bbuf.at[src, rows], bbuf.at[dst, rows], bs_sem.at[sends, k], br_sem.at[dst, k], device)

    own_up = [b_copy(0, 2, k, up, 0) for k in range(PIECES)]
    own_down = [b_copy(0, 3, k, down, 1) for k in range(PIECES)]
    own_pair = [b_copy(0, 1, k, pair, 2) for k in range(PIECES)]
    pair_up = [b_copy(1, 4, k, up, 3) for k in range(PIECES)]
    pair_down = [b_copy(1, 5, k, down, 4) for k in range(PIECES)]
    half = PIECES // 2
    on_own = [b_copy(2, 6, k, up, 5) if k < half else b_copy(3, 6, k, down, 5) for k in range(PIECES)]
    on_pair = [b_copy(4, 7, k, up, 6) if k < half else b_copy(5, 7, k, down, 6) for k in range(PIECES)]

    left = lax.broadcasted_iota(jnp.int32, (1, 128), 1) < BLOCK

    def weight(first, second):
        return jnp.where(left, first, second).astype(jnp.float32)

    per = chunk // BLOCK
    for k in order:
        b_load(k).wait()

        def mask_rows(j, _):
            rows = pl.ds(pl.multiple_of(j * BLOCK, BLOCK), BLOCK)
            for l in range(width // 128):
                cols = pl.ds(l * 128, 128)
                bbuf[0, rows, cols] = bbuf[0, rows, cols] * weight(bocc[2 * l, j], bocc[2 * l + 1, j])
            return _

        lax.fori_loop(k * per, (k + 1) * per, mask_rows, 0)
        own_pair[k].start()
        own_up[k].start()
        own_down[k].start()

    def a_copy(offset):
        i, j = place(offset), place(opposite(offset))
        return remote(astage.at[i], arecv.at[j], as_sem.at[i], ar_sem.at[j], (row_of(offset), c))

    def split(values, i):
        high = values.astype(jnp.bfloat16)
        rows = pl.ds(i * BLOCK, BLOCK)
        ahi[rows, :] = high
        alo[rows, :] = (values - high.astype(jnp.float32)).astype(jnp.bfloat16)

    for j, (ez, eh) in enumerate(chips):
        a_load(j).wait()
        raw = araw.at[j % SLOTS].reshape(BLOCK * 2 * strips, 128)
        for ec in (1, 0):
            offset = (ez, eh, ec)
            i, row = place(offset), row_of(offset)
            first = row * (depth // BLOCK)
            weights = [weight(aocc[0, first + 2 * l], aocc[0, first + 2 * l + 1]) for l in range(strips)]

            def strip(g, _):
                rows = pl.ds(pl.multiple_of(g * 8, 8), 8)
                start = g * (16 * strips) + (row % 2) * strips
                for l in range(strips):
                    astage[i, rows, pl.ds(l * 128, 128)] = raw[pl.ds(start + l, 8, stride=2 * strips), :] * weights[l]
                return _

            lax.fori_loop(0, BLOCK // 8, strip, 0)
            if i == 0:
                split(astage[0], 0)
            elif eh == 0:
                a_copy(offset).start()
        if j + SLOTS < len(chips):
            a_load(j + SLOTS).start()

    for offset in OFFSETS[1:8]:
        a_copy(offset).wait_send()
    for offset in sorted(OFFSETS[8:], key=lambda o: -o[0] % 4 == 2):
        a_copy(offset).start()

    def take(h):
        for offset in OFFSETS:
            i = place(offset)
            if i > 0 and offset[1] == h:
                a_copy(opposite(offset)).wait_recv()
                split(arecv[i], i)

    def multiply(t):
        n, h = TASKS[t]
        slot = t % 2
        if t >= 2:
            c_copy(t - 2).wait_send()

        def convert(j, _):
            rows = pl.ds(pl.multiple_of(j * BLOCK, BLOCK), BLOCK)
            values = bbuf[n, rows, :]
            high = values.astype(jnp.bfloat16)
            bhi[rows, :] = high
            blo[rows, :] = (values - high.astype(jnp.float32)).astype(jnp.bfloat16)
            return _

        lax.fori_loop(0, depth // BLOCK, convert, 0)

        def tile(m, _):
            rows = pl.ds(pl.multiple_of(h * 512 + m * 256, 256), 256)
            high, low = ahi[rows, :], alo[rows, :]
            total = jnp.dot(low, bhi[...], preferred_element_type=jnp.float32)
            total += jnp.dot(high, blo[...], preferred_element_type=jnp.float32)
            total += jnp.dot(high, bhi[...], preferred_element_type=jnp.float32)
            cpart[slot, pl.ds(m * 4, 4)] = total.reshape(4, BLOCK, width)
            return _

        lax.fori_loop(0, 2, tile, 0)
        c_copy(t).start()

    other = (row_of((0, 0, 1)), c)

    def c_copy(t):
        return remote(cpart.at[t % 2, pl.ds(4, 4)], crecv.at[t], cs_sem.at[t], cr_sem.at[t], other)

    ahead, behind = (row_of((1, 0, 0)), c), (row_of((3, 0, 0)), c)

    def z_copy(t, k):
        low, high = pl.ds(0, BLOCK // 2), pl.ds(BLOCK // 2, BLOCK // 2)
        src, dst, device = [
            (crecv.at[t, 2, low], zrecv.at[t, 0, low], ahead),
            (crecv.at[t, 2, high], zrecv.at[t, 0, high], behind),
            (crecv.at[t, 1], zrecv.at[t, 1], ahead),
            (crecv.at[t, 3], zrecv.at[t, 2], behind),
        ][k]
        return remote(src, dst, zs_sem.at[t, k], zr_sem.at[t, k], device)

    def x_copy(t):
        n = TASKS[t][0]
        return remote(keep.at[1, n], xrecv.at[n], xs_sem.at[n], xr_sem.at[n], (row_of((0, 1, 0)), c))

    def over_cores(t):
        c_copy(t).wait_recv()
        crecv[t, 2] = crecv[t, 2] + cpart[t % 2, 2]
        z_copy(t, 0).start()
        z_copy(t, 1).start()
        for ez in (1, 3, 0):
            crecv[t, ez] = crecv[t, ez] + cpart[t % 2, ez]

    def pass_on(t):
        for k, ez, rows in ((0, 1, pl.ds(0, BLOCK // 2)), (1, 3, pl.ds(BLOCK // 2, BLOCK // 2))):
            z_copy(t, k).wait_recv()
            crecv[t, ez, rows, :] = crecv[t, ez, rows, :] + zrecv[t, 0, rows, :]
            z_copy(t, k + 2).start()

    def over_z(t):
        n, h = TASKS[t]
        z_copy(t, 2).wait_recv()
        z_copy(t, 3).wait_recv()
        keep[h, n] = crecv[t, 0] + (zrecv[t, 1] + zrecv[t, 2])
        if h == 1:
            x_copy(t).start()

    def finish(t):
        n, _ = TASKS[t]
        if n not in [task[0] for task in TASKS[:t]]:
            return
        x_copy(t).wait_recv()
        cols = pl.ds(pl.multiple_of(col_of(*PANELS[n]) * width, 128), width)
        out_ref[:, cols] = keep[0, n] + xrecv[n]

    def multiply_last():
        t0 = len(TASKS) - 2
        n = TASKS[t0][0]
        for t in (t0 - 2, t0 - 1):
            c_copy(t).wait_send()
        for step, k in enumerate(order):
            on_pair[k].wait_recv()
            ks = pl.ds(k * chunk, chunk)
            values = bbuf[n, ks, :]
            high = values.astype(jnp.bfloat16)
            bhi[ks, :] = high
            blo[ks, :] = (values - high.astype(jnp.float32)).astype(jnp.bfloat16)
            for t in (t0, t0 + 1):
                h = TASKS[t][1]

                def tile(m, _):
                    rows = pl.ds(pl.multiple_of(h * 512 + m * 256, 256), 256)
                    high, low = ahi[rows, ks], alo[rows, ks]
                    total = jnp.dot(low, bhi[ks, :], preferred_element_type=jnp.float32)
                    total += jnp.dot(high, blo[ks, :], preferred_element_type=jnp.float32)
                    total += jnp.dot(high, bhi[ks, :], preferred_element_type=jnp.float32)
                    total = total.reshape(4, BLOCK, width)
                    if step > 0:
                        total += cpart[t % 2, pl.ds(m * 4, 4)]
                    cpart[t % 2, pl.ds(m * 4, 4)] = total
                    return _

                lax.fori_loop(0, 2, tile, 0)
                if step == PIECES - 1:
                    c_copy(t).start()

    def forward_own():
        for k in (0, 2, 1, 3):
            (own_up if k < half else own_down)[k].wait_recv()
            on_own[k].start()

    def forward_pair():
        for k in order:
            own_pair[k].wait_recv()
            pair_up[k].start()
            pair_down[k].start()

    def pass_on_pair(ks):
        for k in ks:
            (pair_up if k < half else pair_down)[k].wait_recv()
            on_pair[k].start()

    def rest(copies, ks):
        for k in ks:
            copies[k].wait_recv()

    count = len(TASKS)
    done = set()

    def advance(stage, t):
        if (stage, t) not in done:
            done.add((stage, t))
            stage(t)

    def flush(end):
        for stage in (over_cores, pass_on, over_z, finish):
            for t in range(end):
                advance(stage, t)

    before = {
        0: lambda: take(0),
        1: lambda: (forward_own(), forward_pair(), rest(own_up, range(half, PIECES)), rest(own_down, range(half))),
        4: lambda: (flush(4), rest(on_own, range(PIECES))),
        5: lambda: (flush(5), take(1)),
        8: lambda: pass_on_pair((0, 2, 1, 3)),
        10: lambda: rest(pair_up, range(half, PIECES)),
        12: lambda: rest(pair_down, range(half)),
        14: lambda: (advance(over_cores, 13), multiply_last()),
    }
    lags = ((X_LAG, finish), (Z_LAG, over_z), (PASS_LAG, pass_on), (CORE_LAG, over_cores))
    for t in range(count + X_LAG):
        if t in before:
            before[t]()
        if t < count - 2:
            multiply(t)
        for lag, stage in lags:
            if 0 <= t - lag < count:
                advance(stage, t - lag)

    for copies in (own_up, own_down, own_pair, pair_up, pair_down, on_own, on_pair):
        for copy in copies:
            copy.wait_send()
    for offset in OFFSETS[8:]:
        a_copy(offset).wait_send()
    for t in (count - 2, count - 1):
        c_copy(t).wait_send()
    for t in range(count):
        for k in range(4):
            z_copy(t, k).wait_send()
        if TASKS[t][1] == 1:
            x_copy(t).wait_send()


def on_device(tensor, occupancy, coefficients, coeff_occupancy):
    mu_dev, p_dev, nu_all = tensor.shape
    depth, width = coefficients.shape
    count = nu_all // depth
    panels, tasks = len(PANELS), len(TASKS)
    f32, bf16, dma = jnp.float32, jnp.bfloat16, pltpu.SemaphoreType.DMA
    vmem, hbm = pl.BlockSpec(memory_space=pltpu.VMEM), pl.BlockSpec(memory_space=pl.ANY)
    smem = pl.BlockSpec(memory_space=pltpu.SMEM)
    result = pl.pallas_call(
        kernel,
        out_shape=jax.ShapeDtypeStruct((mu_dev, panels * width), f32),
        in_specs=[hbm, smem, hbm, smem],
        out_specs=vmem,
        scratch_shapes=[
            pltpu.VMEM((SLOTS, mu_dev, 2 * depth // 128, 128), f32),
            pltpu.VMEM((count, mu_dev, depth), f32),
            pltpu.VMEM((count, mu_dev, depth), f32),
            pltpu.VMEM((count * mu_dev, depth), bf16),
            pltpu.VMEM((count * mu_dev, depth), bf16),
            pltpu.VMEM((panels, depth, width), f32),
            pltpu.VMEM((depth, width), bf16),
            pltpu.VMEM((depth, width), bf16),
            pltpu.VMEM((2, 8, mu_dev, width), f32),
            pltpu.VMEM((tasks, 4, mu_dev, width), f32),
            pltpu.VMEM((tasks, 3, mu_dev, width), f32),
            pltpu.VMEM((2, panels, mu_dev, width), f32),
            pltpu.VMEM((panels, mu_dev, width), f32),
            dma((count,)), dma((count,)), dma((count,)),
            dma((PIECES,)), dma((7, PIECES)), dma((panels, PIECES)),
            dma((tasks,)), dma((tasks,)), dma((tasks, 4)), dma((tasks, 4)),
            dma((panels,)), dma((panels,)),
        ],
        compiler_params=pltpu.CompilerParams(
            collective_id=0, has_side_effects=True, vmem_limit_bytes=62 * 1024 * 1024),
        cost_estimate=pl.CostEstimate(
            flops=6 * count * mu_dev * depth * panels * width, bytes_accessed=16 * 1024 * 1024, transcendentals=0),
        name="transform",
    )(tensor.reshape(mu_dev, nu_all // 128, 128), occupancy.reshape(1, nu_all // BLOCK), coefficients, coeff_occupancy.T)
    return result.reshape(mu_dev, p_dev, panels * width)


def solution(mesh):
    in_specs = (P("row", "col", None), P("row", "col", None), P("row", "col"), P("row", "col"))
    out_specs = P("row", "col", None)
    return jax.shard_map(
        on_device, mesh=mesh, in_specs=in_specs, out_specs=out_specs, check_vma=False
    )
```

```python
import functools

import jax
import jax.numpy as jnp
from jax import lax
from jax.experimental import pallas as pl
from jax.experimental.pallas import tpu as pltpu
from jax.sharding import PartitionSpec as P

BLOCK = 64
MESH = pl.DeviceIdType.MESH
PIECES = 4
SLOTS = 3
CORE_LAG = 1
PASS_LAG = 3
Z_LAG = 5
X_LAG = 7
OFFSETS = [(ez, eh, ec) for eh in range(2) for ec in range(2) for ez in range(4)]
PANELS = [(0, 0), (0, 1), (3, 0), (1, 0), (3, 1), (1, 1), (2, 0), (2, 1)]
TASKS = [(0, 0), (2, 0), (3, 0), (1, 0), (6, 0), (6, 1), (0, 1), (2, 1), (3, 1), (1, 1),
         (4, 0), (4, 1), (5, 0), (5, 1), (7, 1), (7, 0)]


def place(offset):
    ez, eh, ec = offset
    return eh * 8 + ec * 4 + ez


def opposite(offset):
    ez, eh, ec = offset
    return ((4 - ez) % 4, eh, ec)


def kernel(a_hbm, aocc, b_hbm, bocc, out_ref, araw, astage, arecv, ahi, alo, bbuf, bhi, blo, cpart, crecv, zrecv, keep, xrecv,
           al_sem, as_sem, ar_sem, bl_sem, bs_sem, br_sem, cs_sem, cr_sem, zs_sem, zr_sem, xs_sem, xr_sem):
    depth, width = bbuf.shape[1:]
    chunk = depth // PIECES
    r, c = lax.axis_index("row"), lax.axis_index("col")
    z, xh, core = r // 4, (r // 2) % 2, r % 2
    y, xl = c // 2, c % 2

    def row_of(offset):
        ez, eh, ec = offset
        return ((z + ez) % 4) * 4 + ((xh + eh) % 2) * 2 + (core + ec) % 2

    def col_of(ey, el):
        return ((y + ey) % 4) * 2 + (xl + el) % 2

    def remote(src, dst, send, recv, device):
        return pltpu.make_async_remote_copy(src_ref=src, dst_ref=dst, send_sem=send, recv_sem=recv,
                                            device_id=device, device_id_type=MESH)

    up, down, pair = (r, col_of(1, 0)), (r, col_of(3, 0)), (r, col_of(0, 1))

    def b_load(k):
        rows = pl.ds(k * chunk, chunk)
        return pltpu.make_async_copy(b_hbm.at[rows], bbuf.at[0, rows], bl_sem.at[k])

    strips = depth // 128
    chips = [(2, 0), (1, 0), (3, 0), (0, 0), (2, 1), (1, 1), (3, 1), (0, 1)]

    def a_load(j):
        ez, eh = chips[j]
        rows = pl.ds(pl.multiple_of(row_of((ez, eh, 0)) // 2 * 2 * strips, 8), 2 * strips)
        return pltpu.make_async_copy(a_hbm.at[:, rows], araw.at[j % SLOTS], al_sem.at[j])

    order = (0, 2, 1, 3)
    for k in order:
        b_load(k).start()
    for j in range(SLOTS):
        a_load(j).start()

    barrier = pltpu.get_barrier_semaphore()
    partners = [(row_of(o), c) for o in OFFSETS[1:]] + [up, down, pair]
    for device in partners:
        pl.semaphore_signal(barrier, inc=1, device_id=device, device_id_type=MESH)
    pl.semaphore_wait(barrier, len(partners))

    def b_copy(src, dst, k, device, sends):
        rows = pl.ds(k * chunk, chunk)
        return remote(bbuf.at[src, rows], bbuf.at[dst, rows], bs_sem.at[sends, k], br_sem.at[dst, k], device)

    own_up = [b_copy(0, 2, k, up, 0) for k in range(PIECES)]
    own_down = [b_copy(0, 3, k, down, 1) for k in range(PIECES)]
    own_pair = [b_copy(0, 1, k, pair, 2) for k in range(PIECES)]
    pair_up = [b_copy(1, 4, k, up, 3) for k in range(PIECES)]
    pair_down = [b_copy(1, 5, k, down, 4) for k in range(PIECES)]
    half = PIECES // 2
    on_own = [b_copy(2, 6, k, up, 5) if k < half else b_copy(3, 6, k, down, 5) for k in range(PIECES)]
    on_pair = [b_copy(4, 7, k, up, 6) if k < half else b_copy(5, 7, k, down, 6) for k in range(PIECES)]

    left = lax.broadcasted_iota(jnp.int32, (1, 128), 1) < BLOCK

    def weight(first, second):
        return jnp.where(left, first, second).astype(jnp.float32)

    per = chunk // BLOCK
    for k in order:
        b_load(k).wait()

        def mask_rows(j, _):
            rows = pl.ds(pl.multiple_of(j * BLOCK, BLOCK), BLOCK)
            for l in range(width // 128):
                cols = pl.ds(l * 128, 128)
                bbuf[0, rows, cols] = bbuf[0, rows, cols] * weight(bocc[2 * l, j], bocc[2 * l + 1, j])
            return _

        lax.fori_loop(k * per, (k + 1) * per, mask_rows, 0)
        own_pair[k].start()
        own_up[k].start()
        own_down[k].start()

    def a_copy(offset):
        i, j = place(offset), place(opposite(offset))
        return remote(astage.at[i], arecv.at[j], as_sem.at[i], ar_sem.at[j], (row_of(offset), c))

    def split(values, i):
        high = values.astype(jnp.bfloat16)
        rows = pl.ds(i * BLOCK, BLOCK)
        ahi[rows, :] = high
        alo[rows, :] = (values - high.astype(jnp.float32)).astype(jnp.bfloat16)

    for j, (ez, eh) in enumerate(chips):
        a_load(j).wait()
        raw = araw.at[j % SLOTS].reshape(BLOCK * 2 * strips, 128)
        for ec in (1, 0):
            offset = (ez, eh, ec)
            i, row = place(offset), row_of(offset)
            first = row * (depth // BLOCK)
            weights = [weight(aocc[0, first + 2 * l], aocc[0, first + 2 * l + 1]) for l in range(strips)]

            def strip(g, _):
                rows = pl.ds(pl.multiple_of(g * 8, 8), 8)
                start = g * (16 * strips) + (row % 2) * strips
                for l in range(strips):
                    astage[i, rows, pl.ds(l * 128, 128)] = raw[pl.ds(start + l, 8, stride=2 * strips), :] * weights[l]
                return _

            lax.fori_loop(0, BLOCK // 8, strip, 0)
            if i == 0:
                split(astage[0], 0)
            elif eh == 0:
                a_copy(offset).start()
        if j + SLOTS < len(chips):
            a_load(j + SLOTS).start()

    for offset in OFFSETS[1:8]:
        a_copy(offset).wait_send()
    for offset in sorted(OFFSETS[8:], key=lambda o: -o[0] % 4 == 2):
        a_copy(offset).start()

    def take(h):
        for offset in OFFSETS:
            i = place(offset)
            if i > 0 and offset[1] == h:
                a_copy(opposite(offset)).wait_recv()
                split(arecv[i], i)

    def multiply(t):
        n, h = TASKS[t]
        slot = t % 2
        if t >= 2:
            c_copy(t - 2).wait_send()

        def convert(j, _):
            rows = pl.ds(pl.multiple_of(j * BLOCK, BLOCK), BLOCK)
            values = bbuf[n, rows, :]
            high = values.astype(jnp.bfloat16)
            bhi[rows, :] = high
            blo[rows, :] = (values - high.astype(jnp.float32)).astype(jnp.bfloat16)
            return _

        if t == 0 or TASKS[t - 1][0] != n:
            lax.fori_loop(0, depth // BLOCK, convert, 0)

        def tile(m, _):
            rows = pl.ds(pl.multiple_of(h * 512 + m * 512, 512), 512)
            high, low = ahi[rows, :], alo[rows, :]
            total = jnp.dot(low, bhi[...], preferred_element_type=jnp.float32)
            total += jnp.dot(high, blo[...], preferred_element_type=jnp.float32)
            total += jnp.dot(high, bhi[...], preferred_element_type=jnp.float32)
            cpart[slot, pl.ds(m * 8, 8)] = total.reshape(8, BLOCK, width)
            return _

        tile(0, 0)
        c_copy(t).start()

    other = (row_of((0, 0, 1)), c)

    def c_copy(t):
        return remote(cpart.at[t % 2, pl.ds(4, 4)], crecv.at[t], cs_sem.at[t], cr_sem.at[t], other)

    ahead, behind = (row_of((1, 0, 0)), c), (row_of((3, 0, 0)), c)

    def z_copy(t, k):
        low, high = pl.ds(0, BLOCK // 2), pl.ds(BLOCK // 2, BLOCK // 2)
        src, dst, device = [
            (crecv.at[t, 2, low], zrecv.at[t, 0, low], ahead),
            (crecv.at[t, 2, high], zrecv.at[t, 0, high], behind),
            (crecv.at[t, 1], zrecv.at[t, 1], ahead),
            (crecv.at[t, 3], zrecv.at[t, 2], behind),
        ][k]
        return remote(src, dst, zs_sem.at[t, k], zr_sem.at[t, k], device)

    def x_copy(t):
        n = TASKS[t][0]
        return remote(keep.at[1, n], xrecv.at[n], xs_sem.at[n], xr_sem.at[n], (row_of((0, 1, 0)), c))

    def over_cores(t):
        c_copy(t).wait_recv()
        crecv[t, 2] = crecv[t, 2] + cpart[t % 2, 2]
        z_copy(t, 0).start()
        z_copy(t, 1).start()
        for ez in (1, 3, 0):
            crecv[t, ez] = crecv[t, ez] + cpart[t % 2, ez]

    def pass_on(t):
        for k, ez, rows in ((0, 1, pl.ds(0, BLOCK // 2)), (1, 3, pl.ds(BLOCK // 2, BLOCK // 2))):
            z_copy(t, k).wait_recv()
            crecv[t, ez, rows, :] = crecv[t, ez, rows, :] + zrecv[t, 0, rows, :]
            z_copy(t, k + 2).start()

    def over_z(t):
        n, h = TASKS[t]
        z_copy(t, 2).wait_recv()
        z_copy(t, 3).wait_recv()
        keep[h, n] = crecv[t, 0] + (zrecv[t, 1] + zrecv[t, 2])
        if h == 1:
            x_copy(t).start()

    def finish(t):
        n, _ = TASKS[t]
        if n not in [task[0] for task in TASKS[:t]]:
            return
        x_copy(t).wait_recv()
        cols = pl.ds(pl.multiple_of(col_of(*PANELS[n]) * width, 128), width)
        out_ref[:, cols] = keep[0, n] + xrecv[n]

    def multiply_last():
        t0 = len(TASKS) - 2
        n = TASKS[t0][0]
        for t in (t0 - 2, t0 - 1):
            c_copy(t).wait_send()
        for step, k in enumerate(order):
            on_pair[k].wait_recv()
            ks = pl.ds(k * chunk, chunk)
            values = bbuf[n, ks, :]
            high = values.astype(jnp.bfloat16)
            bhi[ks, :] = high
            blo[ks, :] = (values - high.astype(jnp.float32)).astype(jnp.bfloat16)
            for t in (t0, t0 + 1):
                h = TASKS[t][1]

                def tile(m, _):
                    rows = pl.ds(pl.multiple_of(h * 512 + m * 256, 256), 256)
                    high, low = ahi[rows, ks], alo[rows, ks]
                    total = jnp.dot(low, bhi[ks, :], preferred_element_type=jnp.float32)
                    total += jnp.dot(high, blo[ks, :], preferred_element_type=jnp.float32)
                    total += jnp.dot(high, bhi[ks, :], preferred_element_type=jnp.float32)
                    total = total.reshape(4, BLOCK, width)
                    if step > 0:
                        total += cpart[t % 2, pl.ds(m * 4, 4)]
                    cpart[t % 2, pl.ds(m * 4, 4)] = total
                    return _

                lax.fori_loop(0, 2, tile, 0)
                if step == PIECES - 1:
                    c_copy(t).start()

    def forward_own():
        for k in (0, 2, 1, 3):
            (own_up if k < half else own_down)[k].wait_recv()
            on_own[k].start()

    def forward_pair():
        for k in order:
            own_pair[k].wait_recv()
            pair_up[k].start()
            pair_down[k].start()

    def pass_on_pair(ks):
        for k in ks:
            (pair_up if k < half else pair_down)[k].wait_recv()
            on_pair[k].start()

    def rest(copies, ks):
        for k in ks:
            copies[k].wait_recv()

    count = len(TASKS)
    done = set()

    def advance(stage, t):
        if (stage, t) not in done:
            done.add((stage, t))
            stage(t)

    def flush(end):
        for stage in (over_cores, pass_on, over_z, finish):
            for t in range(end):
                advance(stage, t)

    before = {
        0: lambda: take(0),
        1: lambda: (forward_own(), forward_pair(), rest(own_up, range(half, PIECES)), rest(own_down, range(half))),
        4: lambda: (flush(4), rest(on_own, range(PIECES))),
        5: lambda: (flush(5), take(1)),
        6: lambda: pass_on_pair((0, 2)),
        7: lambda: pass_on_pair((1, 3)),
        10: lambda: rest(pair_up, range(half, PIECES)),
        12: lambda: rest(pair_down, range(half)),
        14: lambda: (advance(over_cores, 13), multiply_last()),
    }
    lags = ((X_LAG, finish), (Z_LAG, over_z), (PASS_LAG, pass_on), (CORE_LAG, over_cores))
    for t in range(count + X_LAG):
        if t in before:
            before[t]()
        if t < count - 2:
            multiply(t)
        for lag, stage in lags:
            if 0 <= t - lag < count:
                advance(stage, t - lag)

    for copies in (own_up, own_down, own_pair, pair_up, pair_down, on_own, on_pair):
        for copy in copies:
            copy.wait_send()
    for offset in OFFSETS[8:]:
        a_copy(offset).wait_send()
    for t in (count - 2, count - 1):
        c_copy(t).wait_send()
    for t in range(count):
        for k in range(4):
            z_copy(t, k).wait_send()
        if TASKS[t][1] == 1:
            x_copy(t).wait_send()


def on_device(tensor, occupancy, coefficients, coeff_occupancy):
    mu_dev, p_dev, nu_all = tensor.shape
    depth, width = coefficients.shape
    count = nu_all // depth
    panels, tasks = len(PANELS), len(TASKS)
    f32, bf16, dma = jnp.float32, jnp.bfloat16, pltpu.SemaphoreType.DMA
    vmem, hbm = pl.BlockSpec(memory_space=pltpu.VMEM), pl.BlockSpec(memory_space=pl.ANY)
    smem = pl.BlockSpec(memory_space=pltpu.SMEM)
    result = pl.pallas_call(
        kernel,
        out_shape=jax.ShapeDtypeStruct((mu_dev, panels * width), f32),
        in_specs=[hbm, smem, hbm, smem],
        out_specs=vmem,
        scratch_shapes=[
            pltpu.VMEM((SLOTS, mu_dev, 2 * depth // 128, 128), f32),
            pltpu.VMEM((count, mu_dev, depth), f32),
            pltpu.VMEM((count, mu_dev, depth), f32),
            pltpu.VMEM((count * mu_dev, depth), bf16),
            pltpu.VMEM((count * mu_dev, depth), bf16),
            pltpu.VMEM((panels, depth, width), f32),
            pltpu.VMEM((depth, width), bf16),
            pltpu.VMEM((depth, width), bf16),
            pltpu.VMEM((2, 8, mu_dev, width), f32),
            pltpu.VMEM((tasks, 4, mu_dev, width), f32),
            pltpu.VMEM((tasks, 3, mu_dev, width), f32),
            pltpu.VMEM((2, panels, mu_dev, width), f32),
            pltpu.VMEM((panels, mu_dev, width), f32),
            dma((count,)), dma((count,)), dma((count,)),
            dma((PIECES,)), dma((7, PIECES)), dma((panels, PIECES)),
            dma((tasks,)), dma((tasks,)), dma((tasks, 4)), dma((tasks, 4)),
            dma((panels,)), dma((panels,)),
        ],
        compiler_params=pltpu.CompilerParams(
            collective_id=0, has_side_effects=True, vmem_limit_bytes=62 * 1024 * 1024),
        cost_estimate=pl.CostEstimate(
            flops=6 * count * mu_dev * depth * panels * width, bytes_accessed=16 * 1024 * 1024, transcendentals=0),
        name="transform",
    )(tensor.reshape(mu_dev, nu_all // 128, 128), occupancy.reshape(1, nu_all // BLOCK), coefficients, coeff_occupancy.T)
    return result.reshape(mu_dev, p_dev, panels * width)


def solution(mesh):
    in_specs = (P("row", "col", None), P("row", "col", None), P("row", "col"), P("row", "col"))
    out_specs = P("row", "col", None)
    return jax.shard_map(
        on_device, mesh=mesh, in_specs=in_specs, out_specs=out_specs, check_vma=False
    )
```

```python
import functools

import jax
import jax.numpy as jnp
from jax import lax
from jax.experimental import pallas as pl
from jax.experimental.pallas import tpu as pltpu
from jax.sharding import PartitionSpec as P

BLOCK = 64
MESH = pl.DeviceIdType.MESH
PIECES = 4
SLOTS = 3
CORE_LAG = 1
PASS_LAG = 3
Z_LAG = 5
X_LAG = 7
OFFSETS = [(ez, eh, ec) for eh in range(2) for ec in range(2) for ez in range(4)]
PANELS = [(0, 0), (0, 1), (3, 0), (1, 0), (3, 1), (1, 1), (2, 0), (2, 1)]
TASKS = [(0, 0), (2, 0), (3, 0), (1, 0), (6, 0), (6, 1), (0, 1), (2, 1), (3, 1), (1, 1),
         (4, 0), (4, 1), (5, 0), (5, 1), (7, 1), (7, 0)]


def place(offset):
    ez, eh, ec = offset
    return eh * 8 + ec * 4 + ez


def opposite(offset):
    ez, eh, ec = offset
    return ((4 - ez) % 4, eh, ec)


def kernel(a_hbm, aocc, b_hbm, bocc, out_ref, araw, astage, arecv, ahi, alo, bbuf, bhi, blo, cpart, crecv, zrecv, keep, xrecv,
           al_sem, as_sem, ar_sem, bl_sem, bs_sem, br_sem, cs_sem, cr_sem, zs_sem, zr_sem, xs_sem, xr_sem):
    depth, width = bbuf.shape[1:]
    chunk = depth // PIECES
    r, c = lax.axis_index("row"), lax.axis_index("col")
    z, xh, core = r // 4, (r // 2) % 2, r % 2
    y, xl = c // 2, c % 2

    def row_of(offset):
        ez, eh, ec = offset
        return ((z + ez) % 4) * 4 + ((xh + eh) % 2) * 2 + (core + ec) % 2

    def col_of(ey, el):
        return ((y + ey) % 4) * 2 + (xl + el) % 2

    def remote(src, dst, send, recv, device):
        return pltpu.make_async_remote_copy(src_ref=src, dst_ref=dst, send_sem=send, recv_sem=recv,
                                            device_id=device, device_id_type=MESH)

    up, down, pair = (r, col_of(1, 0)), (r, col_of(3, 0)), (r, col_of(0, 1))

    def b_load(k):
        rows = pl.ds(k * chunk, chunk)
        return pltpu.make_async_copy(b_hbm.at[rows], bbuf.at[0, rows], bl_sem.at[k])

    strips = depth // 128
    chips = [(2, 0), (1, 0), (3, 0), (0, 0), (2, 1), (1, 1), (3, 1), (0, 1)]

    def a_load(j):
        ez, eh = chips[j]
        rows = pl.ds(pl.multiple_of(row_of((ez, eh, 0)) // 2 * 2 * strips, 8), 2 * strips)
        return pltpu.make_async_copy(a_hbm.at[:, rows], araw.at[j % SLOTS], al_sem.at[j])

    order = (0, 2, 1, 3)
    for k in order:
        b_load(k).start()
    for j in range(SLOTS):
        a_load(j).start()

    barrier = pltpu.get_barrier_semaphore()
    partners = [(row_of(o), c) for o in OFFSETS[1:]] + [up, down, pair]
    for device in partners:
        pl.semaphore_signal(barrier, inc=1, device_id=device, device_id_type=MESH)
    pl.semaphore_wait(barrier, len(partners))

    def b_copy(src, dst, k, device, sends):
        rows = pl.ds(k * chunk, chunk)
        return remote(bbuf.at[src, rows], bbuf.at[dst, rows], bs_sem.at[sends, k], br_sem.at[dst, k], device)

    own_up = [b_copy(0, 2, k, up, 0) for k in range(PIECES)]
    own_down = [b_copy(0, 3, k, down, 1) for k in range(PIECES)]
    own_pair = [b_copy(0, 1, k, pair, 2) for k in range(PIECES)]
    pair_up = [b_copy(1, 4, k, up, 3) for k in range(PIECES)]
    pair_down = [b_copy(1, 5, k, down, 4) for k in range(PIECES)]
    half = PIECES // 2
    on_own = [b_copy(2, 6, k, up, 5) if k < half else b_copy(3, 6, k, down, 5) for k in range(PIECES)]
    on_pair = [b_copy(4, 7, k, up, 6) if k < half else b_copy(5, 7, k, down, 6) for k in range(PIECES)]

    left = lax.broadcasted_iota(jnp.int32, (1, 128), 1) < BLOCK

    def weight(first, second):
        return jnp.where(left, first, second).astype(jnp.float32)

    per = chunk // BLOCK
    for k in order:
        b_load(k).wait()

        def mask_rows(j, _):
            rows = pl.ds(pl.multiple_of(j * BLOCK, BLOCK), BLOCK)
            for l in range(width // 128):
                cols = pl.ds(l * 128, 128)
                bbuf[0, rows, cols] = bbuf[0, rows, cols] * weight(bocc[2 * l, j], bocc[2 * l + 1, j])
            return _

        lax.fori_loop(k * per, (k + 1) * per, mask_rows, 0)
        own_pair[k].start()
        own_up[k].start()
        own_down[k].start()

    def a_copy(offset):
        i, j = place(offset), place(opposite(offset))
        return remote(astage.at[i], arecv.at[j], as_sem.at[i], ar_sem.at[j], (row_of(offset), c))

    def split(values, i):
        high = values.astype(jnp.bfloat16)
        rows = pl.ds(i * BLOCK, BLOCK)
        ahi[rows, :] = high
        alo[rows, :] = (values - high.astype(jnp.float32)).astype(jnp.bfloat16)

    for j, (ez, eh) in enumerate(chips):
        a_load(j).wait()
        raw = araw.at[j % SLOTS].reshape(BLOCK * 2 * strips, 128)
        for ec in (1, 0):
            offset = (ez, eh, ec)
            i, row = place(offset), row_of(offset)
            first = row * (depth // BLOCK)
            weights = [weight(aocc[0, first + 2 * l], aocc[0, first + 2 * l + 1]) for l in range(strips)]

            def strip(g, _):
                rows = pl.ds(pl.multiple_of(g * 8, 8), 8)
                start = g * (16 * strips) + (row % 2) * strips
                for l in range(strips):
                    astage[i, rows, pl.ds(l * 128, 128)] = raw[pl.ds(start + l, 8, stride=2 * strips), :] * weights[l]
                return _

            lax.fori_loop(0, BLOCK // 8, strip, 0)
            if i == 0:
                split(astage[0], 0)
            elif eh == 0:
                a_copy(offset).start()
        if j + SLOTS < len(chips):
            a_load(j + SLOTS).start()

    for offset in OFFSETS[1:8]:
        a_copy(offset).wait_send()
    for offset in sorted(OFFSETS[8:], key=lambda o: -o[0] % 4 == 2):
        a_copy(offset).start()

    def take(h):
        for offset in OFFSETS:
            i = place(offset)
            if i > 0 and offset[1] == h:
                a_copy(opposite(offset)).wait_recv()
                split(arecv[i], i)

    def multiply(t):
        n, h = TASKS[t]
        slot = t % 2
        if t >= 2:
            c_copy(t - 2).wait_send()

        def convert(j, _):
            rows = pl.ds(pl.multiple_of(j * BLOCK, BLOCK), BLOCK)
            values = bbuf[n, rows, :]
            high = values.astype(jnp.bfloat16)
            bhi[rows, :] = high
            blo[rows, :] = (values - high.astype(jnp.float32)).astype(jnp.bfloat16)
            return _

        if t == 0 or TASKS[t - 1][0] != n:
            lax.fori_loop(0, depth // BLOCK, convert, 0)

        def tile(m, _):
            rows = pl.ds(pl.multiple_of(h * 512 + m * 512, 512), 512)
            high, low = ahi[rows, :], alo[rows, :]
            total = jnp.dot(low, bhi[...], preferred_element_type=jnp.float32)
            total += jnp.dot(high, blo[...], preferred_element_type=jnp.float32)
            total += jnp.dot(high, bhi[...], preferred_element_type=jnp.float32)
            cpart[slot, pl.ds(m * 8, 8)] = total.reshape(8, BLOCK, width)
            return _

        tile(0, 0)
        c_copy(t).start()

    other = (row_of((0, 0, 1)), c)

    def c_copy(t):
        return remote(cpart.at[t % 2, pl.ds(4, 4)], crecv.at[t], cs_sem.at[t], cr_sem.at[t], other)

    ahead, behind = (row_of((1, 0, 0)), c), (row_of((3, 0, 0)), c)

    def z_copy(t, k):
        low, high = pl.ds(0, BLOCK // 2), pl.ds(BLOCK // 2, BLOCK // 2)
        src, dst, device = [
            (crecv.at[t, 2, low], zrecv.at[t, 0, low], ahead),
            (crecv.at[t, 2, high], zrecv.at[t, 0, high], behind),
            (crecv.at[t, 1], zrecv.at[t, 1], ahead),
            (crecv.at[t, 3], zrecv.at[t, 2], behind),
        ][k]
        return remote(src, dst, zs_sem.at[t, k], zr_sem.at[t, k], device)

    def x_copy(t):
        n = TASKS[t][0]
        return remote(keep.at[1, n], xrecv.at[n], xs_sem.at[n], xr_sem.at[n], (row_of((0, 1, 0)), c))

    def over_cores(t):
        c_copy(t).wait_recv()
        crecv[t, 2] = crecv[t, 2] + cpart[t % 2, 2]
        z_copy(t, 0).start()
        z_copy(t, 1).start()
        for ez in (1, 3, 0):
            crecv[t, ez] = crecv[t, ez] + cpart[t % 2, ez]

    def pass_on(t):
        for k, ez, rows in ((0, 1, pl.ds(0, BLOCK // 2)), (1, 3, pl.ds(BLOCK // 2, BLOCK // 2))):
            z_copy(t, k).wait_recv()
            crecv[t, ez, rows, :] = crecv[t, ez, rows, :] + zrecv[t, 0, rows, :]
            z_copy(t, k + 2).start()

    def over_z(t):
        n, h = TASKS[t]
        z_copy(t, 2).wait_recv()
        z_copy(t, 3).wait_recv()
        keep[h, n] = crecv[t, 0] + (zrecv[t, 1] + zrecv[t, 2])
        if h == 1:
            x_copy(t).start()

    def finish(t):
        n, _ = TASKS[t]
        if n not in [task[0] for task in TASKS[:t]]:
            return
        x_copy(t).wait_recv()
        values = keep[0, n] + xrecv[n]
        lanes, all_lanes = width // 128, len(PANELS) * width // 128
        for g in range(BLOCK // 8):
            for l in range(lanes):
                rows = pl.ds(g * 8 * all_lanes + col_of(*PANELS[n]) * lanes + l, 8, stride=all_lanes)
                out_ref[rows, :] = values[g * 8:(g + 1) * 8, l * 128:(l + 1) * 128]

    def multiply_last():
        t0 = len(TASKS) - 2
        n = TASKS[t0][0]
        for t in (t0 - 2, t0 - 1):
            c_copy(t).wait_send()
        for step, k in enumerate(order):
            on_pair[k].wait_recv()
            ks = pl.ds(k * chunk, chunk)
            values = bbuf[n, ks, :]
            high = values.astype(jnp.bfloat16)
            bhi[ks, :] = high
            blo[ks, :] = (values - high.astype(jnp.float32)).astype(jnp.bfloat16)
            for t in (t0, t0 + 1):
                h = TASKS[t][1]

                def tile(m, _):
                    rows = pl.ds(pl.multiple_of(h * 512 + m * 256, 256), 256)
                    high, low = ahi[rows, ks], alo[rows, ks]
                    total = jnp.dot(low, bhi[ks, :], preferred_element_type=jnp.float32)
                    total += jnp.dot(high, blo[ks, :], preferred_element_type=jnp.float32)
                    total += jnp.dot(high, bhi[ks, :], preferred_element_type=jnp.float32)
                    total = total.reshape(4, BLOCK, width)
                    if step > 0:
                        total += cpart[t % 2, pl.ds(m * 4, 4)]
                    cpart[t % 2, pl.ds(m * 4, 4)] = total
                    return _

                lax.fori_loop(0, 2, tile, 0)
                if step == PIECES - 1:
                    c_copy(t).start()

    def forward_own():
        for k in (0, 2, 1, 3):
            (own_up if k < half else own_down)[k].wait_recv()
            on_own[k].start()

    def forward_pair():
        for k in order:
            own_pair[k].wait_recv()
            pair_up[k].start()
            pair_down[k].start()

    def pass_on_pair(ks):
        for k in ks:
            (pair_up if k < half else pair_down)[k].wait_recv()
            on_pair[k].start()

    def rest(copies, ks):
        for k in ks:
            copies[k].wait_recv()

    count = len(TASKS)
    done = set()

    def advance(stage, t):
        if (stage, t) not in done:
            done.add((stage, t))
            stage(t)

    def flush(end):
        for stage in (over_cores, pass_on, over_z, finish):
            for t in range(end):
                advance(stage, t)

    before = {
        0: lambda: take(0),
        1: lambda: (forward_own(), forward_pair(), rest(own_up, range(half, PIECES)), rest(own_down, range(half))),
        4: lambda: (flush(4), rest(on_own, range(PIECES))),
        5: lambda: (flush(5), take(1)),
        6: lambda: pass_on_pair((0, 2)),
        7: lambda: pass_on_pair((1, 3)),
        10: lambda: rest(pair_up, range(half, PIECES)),
        12: lambda: rest(pair_down, range(half)),
        14: lambda: (advance(over_cores, 13), multiply_last()),
    }
    lags = ((X_LAG, finish), (Z_LAG, over_z), (PASS_LAG, pass_on), (CORE_LAG, over_cores))
    for t in range(count + X_LAG):
        if t in before:
            before[t]()
        if t < count - 2:
            multiply(t)
        for lag, stage in lags:
            if 0 <= t - lag < count:
                advance(stage, t - lag)

    for copies in (own_up, own_down, own_pair, pair_up, pair_down, on_own, on_pair):
        for copy in copies:
            copy.wait_send()
    for offset in OFFSETS[8:]:
        a_copy(offset).wait_send()
    for t in (count - 2, count - 1):
        c_copy(t).wait_send()
    for t in range(count):
        for k in range(4):
            z_copy(t, k).wait_send()
        if TASKS[t][1] == 1:
            x_copy(t).wait_send()


def on_device(tensor, occupancy, coefficients, coeff_occupancy):
    mu_dev, p_dev, nu_all = tensor.shape
    depth, width = coefficients.shape
    count = nu_all // depth
    panels, tasks = len(PANELS), len(TASKS)
    f32, bf16, dma = jnp.float32, jnp.bfloat16, pltpu.SemaphoreType.DMA
    vmem, hbm = pl.BlockSpec(memory_space=pltpu.VMEM), pl.BlockSpec(memory_space=pl.ANY)
    smem = pl.BlockSpec(memory_space=pltpu.SMEM)
    result = pl.pallas_call(
        kernel,
        out_shape=jax.ShapeDtypeStruct((mu_dev * panels * width // 128, 128), f32),
        in_specs=[hbm, smem, hbm, smem],
        out_specs=vmem,
        scratch_shapes=[
            pltpu.VMEM((SLOTS, mu_dev, 2 * depth // 128, 128), f32),
            pltpu.VMEM((count, mu_dev, depth), f32),
            pltpu.VMEM((count, mu_dev, depth), f32),
            pltpu.VMEM((count * mu_dev, depth), bf16),
            pltpu.VMEM((count * mu_dev, depth), bf16),
            pltpu.VMEM((panels, depth, width), f32),
            pltpu.VMEM((depth, width), bf16),
            pltpu.VMEM((depth, width), bf16),
            pltpu.VMEM((2, 8, mu_dev, width), f32),
            pltpu.VMEM((tasks, 4, mu_dev, width), f32),
            pltpu.VMEM((tasks, 3, mu_dev, width), f32),
            pltpu.VMEM((2, panels, mu_dev, width), f32),
            pltpu.VMEM((panels, mu_dev, width), f32),
            dma((count,)), dma((count,)), dma((count,)),
            dma((PIECES,)), dma((7, PIECES)), dma((panels, PIECES)),
            dma((tasks,)), dma((tasks,)), dma((tasks, 4)), dma((tasks, 4)),
            dma((panels,)), dma((panels,)),
        ],
        compiler_params=pltpu.CompilerParams(
            collective_id=0, has_side_effects=True, vmem_limit_bytes=62 * 1024 * 1024),
        cost_estimate=pl.CostEstimate(
            flops=6 * count * mu_dev * depth * panels * width, bytes_accessed=16 * 1024 * 1024, transcendentals=0),
        name="transform",
    )(tensor.reshape(mu_dev, nu_all // 128, 128), occupancy.reshape(1, nu_all // BLOCK), coefficients, coeff_occupancy.T)
    return result.reshape(mu_dev, p_dev, panels * width)


def solution(mesh):
    in_specs = (P("row", "col", None), P("row", "col", None), P("row", "col"), P("row", "col"))
    out_specs = P("row", "col", None)
    return jax.shard_map(
        on_device, mesh=mesh, in_specs=in_specs, out_specs=out_specs, check_vma=False
    )
```
